32 devices in a mesh: win: 2 (over x), seq: 16 (over z, y, core).
Axes of the slice: x: 2, y: 2, z: 4, core: 2. Of those that a mesh axis runs over, the one named last changes fastest.
Arguments:
- code_ids: int32 [4, 2048], P('win', 'seq'), may hold values from 0 to 2047
- conditioning: bfloat16 [4, 2048, 1920], P('win', 'seq'), may hold values from -6 to 6
- code_embedding: bfloat16 [2048, 1920], P(('win', 'seq')), may hold values from -6 to 6
- w_qkv: bfloat16 [1920, 5760], P(('win', 'seq')), may hold values from -0.125 to 0.125
- w_out: bfloat16 [1920, 1920], P(('win', 'seq')), may hold values from -0.375 to 0.375
- w_fc: bfloat16 [1920, 7680], P(('win', 'seq')), may hold values from -0.125 to 0.125
- w_proj: bfloat16 [7680, 1920], P(('win', 'seq')), may hold values from -0.0625 to 0.0625
- norm_gains: bfloat16 [2, 1920], P(None, ('win', 'seq')), may hold values from 0.5 to 1.5
- norm_shifts: bfloat16 [2, 1920], P(None, ('win', 'seq')), may hold values from -3 to 3
- fc_bias: bfloat16 [7680], P(('win', 'seq')), may hold values from -3 to 3
- proj_bias: bfloat16 [1920], P(('win', 'seq')), may hold values from -3 to 3
- cotangent: bfloat16 [4, 2048, 1920], P('win', 'seq'), may hold values from -6 to 6
Outputs:
- layer_out: float32 [4, 2048, 1920], P('win', 'seq')
- grad_conditioning: float32 [4, 2048, 1920], P('win', 'seq')
- grad_embedding: float32 [2048, 1920], P(('win', 'seq'))
- grad_qkv: float32 [1920, 5760], P(('win', 'seq'))
- grad_out: float32 [1920, 1920], P(('win', 'seq'))
- grad_fc: float32 [1920, 7680], P(('win', 'seq'))
- grad_proj: float32 [7680, 1920], P(('win', 'seq'))
- grad_gains: float32 [2, 1920], P(None, ('win', 'seq'))
- grad_shifts: float32 [2, 1920], P(None, ('win', 'seq'))
- grad_fc_bias: float32 [7680], P(('win', 'seq'))
- grad_proj_bias: float32 [1920], P(('win', 'seq'))
The draws below stay inside these ranges and needn't reach their ends.
All inputs are finite; a program needn't handle non-finite values.
Results may differ from the reference program's by a relative error of at most 0.009.
Values may be sent and summed in bfloat16 or wider, within the bound.
No kernel may reach another device: no remote copies, remote signals or barrier semaphores. Data moves between devices by JAX's collectives and lax.ppermute only.
A program may use at most 320 MiB of HBM per device.

```python
import math
import jax
import jax.numpy as jnp
from jax import lax

D = 1920
HEADS = 15
HEAD_DIM = 128
FF = 7680
VOCAB = 2048
BLOCK = 128
WINDOWS = 4
LENGTH = 2048


def plant(drawn, key, smallest, largest):
    index_at = [jax.random.randint(jax.random.fold_in(key, axis), (), 0, length) for axis, length in enumerate(drawn.shape)]
    widest = drawn.shape.index(max(drawn.shape))
    next_to = index_at[:widest] + [(index_at[widest] + 1) % drawn.shape[widest]] + index_at[widest + 1:]
    return drawn.at[tuple(index_at)].set(smallest).at[tuple(next_to)].set(largest)


def block_levels(rng, shape, pieces, smallest, largest):
    def one(dim, blocks):
        steps = jax.random.uniform(jax.random.fold_in(jax.random.fold_in(rng, 6), dim), (blocks,), jnp.float32, smallest / len(pieces), largest / len(pieces))
        return jnp.repeat(jnp.exp(steps), shape[dim] // blocks).reshape((-1,) + (1,) * (len(shape) - dim - 1))

    level = one(*pieces[0])
    for cut in pieces[1:]:
        level = level * one(*cut)
    return level


def normal_values(stream_key, dims, scale, reach, split=(), kind=jnp.bfloat16):
    gain = block_levels(stream_key, dims, split, -0.22, 0.18) if split else 1.0
    values = jax.random.normal(stream_key, dims, jnp.float32) * scale * gain
    return jnp.minimum(jnp.maximum(values, -reach), reach).astype(kind)


def setup_inputs(seed: int = 0) -> dict:
    key_of = jax.random.split(jax.random.key(seed), 13)
    return {
        "code_ids": plant(jax.random.randint(key_of[0], (WINDOWS, LENGTH), 0, VOCAB), jax.random.fold_in(key_of[0], 1), 0, VOCAB - 1).astype(jnp.int32),
        "conditioning": normal_values(key_of[1], (WINDOWS, LENGTH, D), 1.0, 6.0, ((0, 2), (1, 16))),
        "code_embedding": normal_values(key_of[2], (VOCAB, D), 1.0, 6.0, ((0, 32),)),
        "w_qkv": normal_values(key_of[3], (D, 3 * D), D ** -0.5, 0.125, ((0, 32),)),
        "w_out": normal_values(key_of[4], (D, D), (D // 8) ** -0.5, 0.375, ((0, 32),)),
        "w_fc": normal_values(key_of[5], (D, FF), D ** -0.5, 0.125, ((0, 32),)),
        "w_proj": normal_values(key_of[6], (FF, D), FF ** -0.5, 0.0625, ((0, 32),)),
        "norm_gains": jnp.clip(1.0 + 0.1 * jax.random.normal(key_of[7], (2, D), jnp.float32), 0.5, 1.5).astype(jnp.bfloat16),
        "norm_shifts": normal_values(key_of[8], (2, D), 0.5, 3.0, ((1, 32),)),
        "fc_bias": normal_values(key_of[9], (FF,), 0.5, 3.0, ((0, 32),)),
        "proj_bias": normal_values(key_of[10], (D,), 0.5, 3.0, ((0, 32),)),
        "cotangent": normal_values(key_of[11], (WINDOWS, LENGTH, D), 1.0, 6.0, ((0, 2), (1, 16))),
    }


@jax.custom_vjp
def low(v):
    return lax.optimization_barrier(v.astype(jnp.bfloat16)).astype(jnp.float32)

@jax.custom_vjp
def low_back(v):
    return v

def low_keep(v):
    return (low(v), None)

def low_pass(kept, grad):
    return (grad,)

def back_keep(v):
    return (v, None)

def back_low(kept, grad):
    return (low(grad),)
low.defvjp(low_keep, low_pass)
low_back.defvjp(back_keep, back_low)
EPS = 1e-05
HIGH = lax.Precision.HIGHEST

def layer_norm(values, gain_row, shift_row):
    center = values - lax.optimization_barrier(jnp.mean(values, axis=-1, keepdims=True))
    spread = lax.optimization_barrier(jnp.mean(center * center, axis=-1, keepdims=True))
    return center * lax.rsqrt(spread + EPS) * gain_row + shift_row

def matmul(left_side, right_side):
    return jnp.matmul(left_side, right_side, precision=HIGH)

def window_group(weights, codes_part, cond_part):
    embedding, w_qkv, w_out, w_fc, w_proj, norm_gains, norm_shifts, fc_bias, proj_bias = weights
    group_size = codes_part.shape[0]
    window_len = codes_part.shape[1]
    block_rows = window_len // BLOCK
    model_width = w_out.shape[0]
    resid_in = jnp.take(embedding, codes_part, axis=0) + cond_part
    normed = low(layer_norm(resid_in, norm_gains[0], norm_shifts[0]))
    packed = low_back(low(matmul(normed, w_qkv)))
    packed = packed.reshape(group_size, block_rows, BLOCK, 3, HEADS, HEAD_DIM)
    queries = packed[:, :, :, 0]
    key_rows = packed[:, :, :, 1]
    values_all = packed[:, :, :, 2]
    scores = jnp.einsum('grchd,gschd->gchrs', queries, key_rows, precision=HIGH) * (1.0 / math.sqrt(HEAD_DIM))
    scores = low_back(scores)
    causal = jnp.arange(block_rows)[:, None] >= jnp.arange(block_rows)[None, :]
    scores = jnp.where(causal, scores, -1e+30)
    attn_probs = low(jax.nn.softmax(scores, axis=-1))
    attn_mixed = jnp.einsum('gchrs,gschd->grchd', attn_probs, values_all, precision=HIGH)
    attn_mixed = low_back(low(attn_mixed.reshape(group_size, window_len, model_width)))
    resid_mid = resid_in + low_back(matmul(attn_mixed, w_out))
    normed_two = low(layer_norm(resid_mid, norm_gains[1], norm_shifts[1]))
    pre_act = low_back(matmul(normed_two, w_fc) + fc_bias)
    hidden = low(jax.nn.gelu(pre_act, approximate=True))
    return resid_mid + matmul(hidden, w_proj) + proj_bias

def reference(code_ids, conditioning, code_embedding, w_qkv, w_out, w_fc, w_proj, norm_gains, norm_shifts, fc_bias, proj_bias, cotangent):
    windows_all = code_ids.shape[0]
    window_len = code_ids.shape[1]
    group_size = math.gcd(windows_all, max(1, 4096 // window_len))
    group_count = windows_all // group_size
    floats = tuple((array.astype(jnp.float32) for array in (code_embedding, w_qkv, w_out, w_fc, w_proj, norm_gains, norm_shifts, fc_bias, proj_bias)))
    codes_grouped = code_ids.reshape(group_count, group_size, window_len)

    def forward(cond_all, *weights):

        def one_group(parts):
            return jax.checkpoint(window_group)(weights, parts[0], parts[1])
        cond_grouped = cond_all.reshape(group_count, group_size, window_len, cond_all.shape[-1])
        outputs = lax.map(one_group, (codes_grouped, cond_grouped))
        return outputs.reshape(cond_all.shape)
    result, pullback = jax.vjp(forward, conditioning.astype(jnp.float32), *floats)
    gradients = pullback(cotangent.astype(jnp.float32))
    return (result, gradients[0], gradients[1], gradients[2], gradients[3], gradients[4], gradients[5], gradients[6], gradients[7], gradients[8], gradients[9])
```

```python
import math

import jax
import jax.numpy as jnp
from jax import lax
from jax.experimental import pallas as pl
from jax.experimental.pallas import tpu as pltpu
from jax.sharding import Mesh, PartitionSpec as P

HEAD_DIM = 128
EPS = 1e-05
F32 = jnp.float32
BF16 = jnp.bfloat16
SEQ = ("h", "l", "y", "c")
ALL = ("x",) + SEQ


def dot(a, b, dims):
    return lax.dot_general(a, b, (dims, ((), ())), preferred_element_type=F32)


def size(axis):
    return lax.axis_size(axis)


def swap(a, axis):
    return lax.ppermute(a, axis, [(0, 1), (1, 0)])


def pick(a, i, dim):
    return lax.dynamic_index_in_dim(a, i, dim, keepdims=False)


def gather_axis(a, axis):
    if size(axis) != 2:
        return lax.all_gather(a, axis, axis=0, tiled=False)
    got = swap(a, axis)
    first = lax.axis_index(axis) == 0
    return jnp.where(first, jnp.stack([a, got]), jnp.stack([got, a]))


def scatter_axis(a, axis, dim):
    if size(axis) != 2:
        return lax.psum_scatter(a.astype(BF16), axis, scatter_dimension=dim, tiled=False).astype(F32)
    me = lax.axis_index(axis)
    got = swap(pick(a, 1 - me, dim).astype(BF16), axis)
    return pick(a, me, dim).astype(F32) + got.astype(F32)


def gather_rows(block):
    both = gather_axis(block, "h")
    a, b = both[:, 0], both[:, 1]
    a = gather_axis(a, "x")
    b = gather_axis(b, "y")
    a = gather_axis(a, "y")
    b = gather_axis(b, "x")
    a = jnp.transpose(a, (1, 2, 0, 3, 4))
    b = jnp.transpose(b, (0, 2, 1, 3, 4))
    return jnp.stack([a, b], axis=2)


def scatter_rows(grad):
    a, b = grad[:, :, 0], grad[:, :, 1]
    a = scatter_axis(a, "y", 2)
    b = scatter_axis(b, "x", 0)
    a = scatter_axis(a, "x", 0)
    b = scatter_axis(b, "y", 1)
    return scatter_axis(jnp.stack([a, b], axis=1), "h", 0)


def trade(a):
    me = lax.axis_index("c")
    got = swap(pick(a, 1 - me, 1), "c")
    mine = pick(a, me, 1)
    first = me == 0
    a = jnp.where(first, jnp.stack([mine, got], 1), jnp.stack([got, mine], 1))
    me = lax.axis_index("l")
    got = swap(pick(a, 1 - me, 0), "l")
    mine = pick(a, me, 0)
    first = me == 0
    return jnp.where(first, jnp.stack([mine, got], 0), jnp.stack([got, mine], 0))


def share(a):
    two = jnp.concatenate([a, swap(a, "l")], axis=0)
    return jnp.concatenate([two, swap(two, "c")], axis=0)


def total(a):
    half = a.shape[0] // 2
    a = a[:half] + swap(a[half:].astype(BF16), "c").astype(F32)
    half = half // 2
    return a[:half] + swap(a[half:].astype(BF16), "l").astype(F32)


def norm_stats(v):
    center = v - jnp.mean(v, axis=-1, keepdims=True)
    inv = lax.rsqrt(jnp.mean(center * center, axis=-1, keepdims=True) + EPS)
    return center * inv, inv


def norm_back(hat, inv, gain, grad):
    g = grad * gain
    back = inv * (g - jnp.mean(g, axis=-1, keepdims=True) - hat * jnp.mean(g * hat, axis=-1, keepdims=True))
    return back, jnp.sum(grad * hat, axis=0), jnp.sum(grad, axis=0)


def probs_of(q, k, cols):
    n = q.shape[0]
    s = dot(q, k, ((1,), (1,))) * (1.0 / math.sqrt(HEAD_DIM))
    t = lax.broadcasted_iota(jnp.int32, (n, n), 0)
    u = lax.broadcasted_iota(jnp.int32, (n, n), 1)
    keep = (lax.rem(t, cols) == lax.rem(u, cols)) & (t >= u)
    s = jnp.where(keep, s, -1e30)
    e = jnp.exp(s - jnp.max(s, axis=-1, keepdims=True))
    return e / jnp.sum(e, axis=-1, keepdims=True)


def head_slices(h, heads):
    return [slice((p * heads + h) * HEAD_DIM, (p * heads + h + 1) * HEAD_DIM) for p in range(3)]


def attend_kernel(heads, cols, packed_ref, out_ref):
    for h in range(heads):
        sq, sk, sv = head_slices(h, heads)
        p = probs_of(packed_ref[:, sq], packed_ref[:, sk], cols)
        out_ref[:, sq] = dot(p.astype(BF16), packed_ref[:, sv], ((1,), (0,))).astype(BF16)


def attend_back_kernel(heads, cols, packed_ref, grad_ref, out_ref):
    scale = 1.0 / math.sqrt(HEAD_DIM)
    for h in range(heads):
        sq, sk, sv = head_slices(h, heads)
        q, k, v, g = packed_ref[:, sq], packed_ref[:, sk], packed_ref[:, sv], grad_ref[:, sq]
        p = probs_of(q, k, cols)
        out_ref[:, sv] = dot(p.astype(BF16), g, ((0,), (0,))).astype(BF16)
        dp = dot(g, v, ((1,), (1,)))
        ds = (p * (dp - jnp.sum(p * dp, axis=-1, keepdims=True))).astype(BF16)
        out_ref[:, sq] = (dot(ds, k, ((1,), (0,))) * scale).astype(BF16)
        out_ref[:, sk] = (dot(ds, q, ((0,), (0,))) * scale).astype(BF16)


def attention(kernel, heads, cols, chunk, out_cols, *arrays):
    tokens = arrays[0].shape[0]
    steps = tokens // chunk
    return pl.pallas_call(
        lambda *refs: kernel(heads, cols, *refs),
        grid=(steps,),
        in_specs=[pl.BlockSpec((chunk, a.shape[1]), lambda i: (i, 0)) for a in arrays],
        out_specs=pl.BlockSpec((chunk, out_cols), lambda i: (i, 0)),
        out_shape=jax.ShapeDtypeStruct((tokens, out_cols), BF16),
        compiler_params=pltpu.CompilerParams(vmem_limit_bytes=32 * 2**20),
        cost_estimate=pl.CostEstimate(flops=tokens * chunk * out_cols * 4, bytes_accessed=tokens * out_cols * 8, transcendentals=0),
    )(*arrays)


def gelu_parts(v):
    k = math.sqrt(2.0 / math.pi)
    th = jnp.tanh(k * (v + 0.044715 * v * v * v))
    value = 0.5 * v * (1.0 + th)
    slope = 0.5 * (1.0 + th) + 0.5 * v * (1.0 - th * th) * k * (1.0 + 3 * 0.044715 * v * v)
    return value, slope


def shards(code_ids, conditioning, code_embedding, w_qkv, w_out, w_fc, w_proj, norm_gains, norm_shifts, fc_bias, proj_bias, cotangent):
    nx, nh, ns = size("x"), size("h"), size("h") * 8
    wins, block_len = code_ids.shape
    cols = block_len // ns
    width = conditioning.shape[2]
    tokens = wins * block_len
    chunk = ns * cols
    rows = w_qkv.shape[0]
    ff_rows = w_proj.shape[0]
    emb_rows = code_embedding.shape[0]
    ff = w_fc.shape[1]
    ff_part = ff // 4
    heads = -(-(width // HEAD_DIM) // 4)
    hw = heads * HEAD_DIM
    pad = 4 * hw - width
    me_l, me_c = lax.axis_index("l"), lax.axis_index("c")
    me_s = lax.axis_index(SEQ)

    small = jnp.concatenate([norm_gains.reshape(-1), norm_shifts.reshape(-1), proj_bias, fc_bias])
    small = lax.all_gather(small, ALL, axis=0, tiled=False)
    gains = jnp.transpose(small[:, : 2 * rows].reshape(-1, 2, rows), (1, 0, 2)).reshape(2, width).astype(F32)
    shifts = jnp.transpose(small[:, 2 * rows : 4 * rows].reshape(-1, 2, rows), (1, 0, 2)).reshape(2, width).astype(F32)
    proj_b = small[:, 4 * rows : 5 * rows].reshape(width).astype(F32)
    fc_b = small[:, 5 * rows :].reshape(nx, nh, 2, 2, 2, 2, ff_rows // 2)
    fc_b = pick(pick(fc_b, me_c, 4), me_l, 2)
    fc_b = jnp.transpose(fc_b, (0, 1, 3, 2, 4)).reshape(ff_part).astype(F32)
    ids = lax.all_gather(code_ids, SEQ, axis=0, tiled=False)
    ids = jnp.transpose(ids, (1, 0, 2)).reshape(wins, ns, ns, cols)

    def to_columns(a):
        return lax.all_to_all(a[:, None], SEQ, split_axis=2, concat_axis=1, tiled=True).reshape(tokens, width)

    def to_rows(a):
        a = a.reshape(wins, ns, cols, width)
        return lax.all_to_all(a, SEQ, split_axis=1, concat_axis=2, tiled=True).reshape(wins, block_len, width)

    cond = to_columns(conditioning)
    cot = to_columns(cotangent)

    def member_cols(w):
        return jnp.transpose(w.reshape(w.shape[0], 2, 2, -1), (1, 2, 0, 3))

    qkv_w = jnp.pad(w_qkv.reshape(rows, 3, width), ((0, 0), (0, 0), (0, pad))).reshape(rows, 3, 4, hw)
    qkv_w = jnp.transpose(qkv_w, (2, 0, 1, 3)).reshape(2, 2, rows, 3 * hw)
    fc_w = w_fc.reshape(rows, nx, nh, 2, 2, 2, 2, ff_rows // 2)
    fc_w = jnp.transpose(fc_w, (3, 5, 0, 1, 2, 6, 4, 7)).reshape(2, 2, rows, ff_part)
    emb_w = gather_rows(code_embedding.reshape(2, emb_rows // 2, width)).reshape(-1, width)
    qkv_w = gather_rows(trade(qkv_w).reshape(2, 2 * rows, 3 * hw)).reshape(width, 3 * hw)
    out_w = gather_rows(trade(member_cols(w_out)).reshape(2, 2 * rows, width // 4)).reshape(width, width // 4)
    out_w = trade(jnp.pad(out_w, ((0, pad), (0, 0))).reshape(2, 2, hw, width // 4))
    out_w = jnp.transpose(out_w, (2, 0, 1, 3)).reshape(hw, width)
    fc_w = gather_rows(trade(fc_w).reshape(2, 2 * rows, ff_part)).reshape(width, ff_part)
    proj_w = gather_rows(w_proj.reshape(2, ff_rows // 2, width)).reshape(ff_part, width)

    s_of = [me_s ^ (dl * 4 + dc) for dc in range(2) for dl in range(2)]
    group_ids = jnp.concatenate([pick(ids, s, 2).reshape(tokens) for s in s_of])
    at = jnp.arange(emb_w.shape[0], dtype=jnp.int32)
    half = emb_rows // 2
    r, at = at % half, at // half
    y, at = at % 2, at // 2
    part, at = at % 2, at // 2
    h, x = at % nh, at // nh
    row_ids = ((((x * nh + h) * 2 + me_l) * 2 + y) * 2 + me_c) * emb_rows + part * half + r
    onehot = (group_ids[:, None] == row_ids[None, :]).astype(BF16)
    emb = total(dot(onehot, emb_w, ((1,), (0,))))
    resid_in = emb + cond.astype(F32)

    hat_one, inv_one = norm_stats(resid_in)
    normed_one = share((hat_one * gains[0] + shifts[0]).astype(BF16))
    packed = dot(normed_one, qkv_w, ((1,), (0,))).astype(BF16)
    mixed = attention(attend_kernel, heads, cols, chunk, hw, packed)
    resid_mid = resid_in + total(dot(mixed, out_w, ((1,), (0,))))

    hat_two, inv_two = norm_stats(resid_mid)
    normed_two = share((hat_two * gains[1] + shifts[1]).astype(BF16))
    pre_act = dot(normed_two, fc_w, ((1,), (0,))) + fc_b
    value, slope = gelu_parts(pre_act)
    hidden = value.astype(BF16)
    layer_out = resid_mid + total(dot(hidden, proj_w, ((1,), (0,)))) + proj_b
    layer_out = to_rows(layer_out.astype(BF16)).astype(F32)

    cot_all = share(cot)
    grad_proj = dot(hidden, cot_all, ((0,), (0,))).reshape(nx, nh, 2, 2, ff_rows // 2, width)
    grad_proj = scatter_rows(grad_proj).reshape(ff_rows, width)
    cot_f = cot.astype(F32)
    grad_pre = (dot(cot_all, proj_w, ((1,), (1,))) * slope).astype(BF16)
    grad_fcb = jnp.sum(grad_pre.astype(F32), axis=0)
    grad_fc = dot(normed_two, grad_pre, ((0,), (0,))).reshape(nx, nh, 2, 2, 2 * rows, ff_part)
    grad_fc = scatter_rows(grad_fc).astype(BF16)
    grad_fc = trade(grad_fc.reshape(2, 2, rows, ff_part))
    grad_fc = grad_fc.reshape(2, 2, rows, nx, nh, 2, 2, ff_rows // 2)
    grad_fc = jnp.transpose(grad_fc, (2, 3, 4, 0, 6, 1, 5, 7)).reshape(rows, ff).astype(F32)
    grad_two = total(dot(grad_pre, fc_w, ((1,), (1,))))
    back, gain_two, shift_two = norm_back(hat_two, inv_two, gains[1], grad_two)
    grad_mid = cot_f + back

    branch = share(grad_mid.astype(BF16))
    grad_out = dot(mixed, branch, ((0,), (0,))).astype(BF16)
    grad_out = jnp.transpose(grad_out.reshape(hw, 2, 2, width // 4), (1, 2, 0, 3))
    grad_out = trade(grad_out).reshape(4 * hw, width // 4)[:width]
    grad_out = scatter_rows(grad_out.reshape(nx, nh, 2, 2, 2 * rows, width // 4)).astype(BF16)
    grad_out = trade(grad_out.reshape(2, 2, rows, width // 4))
    grad_out = jnp.transpose(grad_out, (2, 0, 1, 3)).reshape(rows, width).astype(F32)
    grad_mixed = dot(branch, out_w, ((1,), (1,))).astype(BF16)
    grad_packed = attention(attend_back_kernel, heads, cols, chunk, 3 * hw, packed, grad_mixed)
    grad_qkv = dot(normed_one, grad_packed, ((0,), (0,))).reshape(nx, nh, 2, 2, 2 * rows, 3 * hw)
    grad_qkv = scatter_rows(grad_qkv).astype(BF16)
    grad_qkv = trade(grad_qkv.reshape(2, 2, rows, 3 * hw))
    grad_qkv = jnp.transpose(grad_qkv.reshape(4, rows, 3, hw), (1, 2, 0, 3)).reshape(rows, 3, 4 * hw)
    grad_qkv = grad_qkv[:, :, :width].reshape(rows, 3 * width).astype(F32)
    grad_one = total(dot(grad_packed, qkv_w, ((1,), (1,))))
    back, gain_one, shift_one = norm_back(hat_one, inv_one, gains[0], grad_one)
    grad_cond = (grad_mid + back).astype(BF16)
    grad_cond_all = share(grad_cond)
    grad_cond = to_rows(grad_cond).astype(F32)
    grad_emb = dot(onehot, grad_cond_all, ((0,), (0,))).reshape(nx, nh, 2, 2, emb_rows // 2, width)
    grad_emb = scatter_rows(grad_emb).reshape(emb_rows, width)

    small = jnp.stack([gain_one, gain_two, shift_one, shift_two, jnp.sum(cot_f, axis=0)])
    small = small.reshape(5, nx, nh, 2, 2, 2, rows)
    small = lax.psum_scatter(small, "c", scatter_dimension=5, tiled=False)
    small = lax.psum_scatter(small, "l", scatter_dimension=3, tiled=False)
    small = jnp.transpose(small, (1, 2, 3, 0, 4)).reshape(nx, nh, 2, 5 * rows)
    grad_fcb = jnp.transpose(grad_fcb.reshape(nx, nh, 2, 2, ff_rows // 2), (0, 1, 3, 2, 4)).reshape(nx, nh, 2, ff_rows)
    small = jnp.concatenate([small, grad_fcb], axis=-1)
    small = lax.psum_scatter(small, "y", scatter_dimension=2, tiled=False)
    small = lax.psum_scatter(small, "x", scatter_dimension=0, tiled=False)
    small = lax.psum_scatter(small, "h", scatter_dimension=0, tiled=False)
    return (
        layer_out,
        grad_cond,
        grad_emb,
        grad_qkv,
        grad_out,
        grad_fc,
        grad_proj,
        small[: 2 * rows].reshape(2, rows),
        small[2 * rows : 4 * rows].reshape(2, rows),
        small[5 * rows :],
        small[4 * rows : 5 * rows],
    )


def solution(mesh):
    seq = mesh.shape["seq"]
    fine = Mesh(mesh.devices.reshape(mesh.shape["win"], seq // 8, 2, 2, 2), ALL)
    every = P(ALL, None)
    part = P(None, ALL)
    token = P("x", SEQ, None)
    return jax.shard_map(
        shards,
        mesh=fine,
        in_specs=(P("x", SEQ), token, every, every, every, every, every, part, part, P(ALL), P(ALL), token),
        out_specs=(token, token, every, every, every, every, every, part, part, P(ALL), P(ALL)),
        check_vma=False,
    )
```
